32 devices in a mesh: prow: 4 (over y, x), pcol: 8 (over z, core).
Axes of the slice: x: 2, y: 2, z: 4, core: 2. Of those that a mesh axis runs over, the one named last changes fastest.
Arguments:
- top_inverse: bfloat16 [8, 8, 256, 256], P('pcol'), may hold values from -3 to 3
- upper_structure: int32 [4, 8], replicated, may hold values from 0 to 1, as said below
- upper_panels: bfloat16 [4, 8, 256, 256], P('prow', 'pcol'), may hold values from -0.375 to 0.375
- upper_diag_inverse: float32 [4, 256, 256], P('prow'), may hold values from -6 to 6
- child_order: int32 [8], replicated, may hold values from 0 to 7, each once
- child_keep: int32 [8, 8], P('prow'), may hold values 0 or 1
- lower_panels: bfloat16 [8, 8, 256, 256], P('prow', 'pcol'), may hold values from -0.25 to 0.25
- parent_panels: bfloat16 [8, 256, 256], P('prow'), may hold values from -0.1875 to 0.1875
- lower_diag_inverse: float32 [8, 256, 256], P('prow'), may hold values from -6 to 6
Outputs:
- upper_blocks: bfloat16 [4, 8, 256, 256], P('prow', 'pcol')
- upper_diag: float32 [4, 256, 256], P('prow')
- lower_blocks: bfloat16 [8, 8, 256, 256], P('prow', 'pcol')
- lower_parent: bfloat16 [8, 256, 256], P('prow')
- lower_diag: float32 [8, 256, 256], P('prow')
The draws below stay inside these ranges and needn't reach their ends.
Inputs may be any that keep to these rules, and one draw needn't show every extreme that they name: `upper_structure`: 1 where top-separator supernode I lies in the block structure of upper-level supernode K, else 0. `child_order`: each number once; lower-level supernode k is a child of upper-level supernode child_order[k] // 2, so every upper-level supernode has exactly 2 children. `child_keep`: 1 where a lower-level supernode keeps a block of its parent's structure.
All inputs are finite; a program needn't handle non-finite values.
Results may differ from the reference program's by a relative error of at most 0.0049.
Values may be sent and summed in bfloat16 or wider, within the bound.
No kernel may reach another device: no remote copies, remote signals or barrier semaphores. Data moves between devices by JAX's collectives and lax.ppermute only.
A program may use at most 128 MiB of HBM per device.

```python
import jax
import jax.numpy as jnp
from jax import lax

S = 256
CH = 2
NT = 8
NK1 = 4
NK2 = 8


def draw_upper_structure(key, part):
    key = jax.random.fold_in(key, 11)
    weight_key, roll_key = jax.random.split(key)
    column_weight = jax.random.randint(weight_key, (NT,), 1, 9)
    rolled = jax.random.randint(roll_key, (NK1, NT), 0, 8)
    return (rolled < column_weight[None, :]).astype(jnp.int32)


def place_ends(entries, stream_key, low, top_value):
    longest = entries.shape.index(max(entries.shape))
    spots = []
    for shift in (0, 1):
        where = [jax.random.randint(jax.random.fold_in(stream_key, axis), (), 0, length) for axis, length in enumerate(entries.shape)]
        where[longest] = (where[longest] + shift) % entries.shape[longest]
        spots.append(tuple(where))
    return entries.at[spots[0]].set(low).at[spots[1]].set(top_value)


def levels(key, dims, cuts, smallest, high):
    factor_of, own = 1.0, jax.random.fold_in(key, 6)
    for dim, blocks in cuts:
        steps = jnp.exp(jax.random.uniform(jax.random.fold_in(own, dim), (blocks,), jnp.float32, smallest / len(cuts), high / len(cuts)))
        factor_of = factor_of * jnp.repeat(steps, dims[dim] // blocks).reshape([-1 if axis == dim else 1 for axis in range(len(dims))])
    return factor_of


def scatter_about(key, dims, scale, most, cuts=(), kind=jnp.bfloat16):
    result = scale * jax.random.normal(key, dims, jnp.float32)
    if cuts:
        result = result * levels(key, dims, cuts, -0.22, 0.18)
    return jnp.clip(result, -most, most).astype(kind)


def setup_inputs(seed: int = 0) -> dict:
    seeds = jax.random.split(jax.random.key(seed), 10)
    top_inverse = scatter_about(seeds[0], (NT, NT, S, S), (NT // 2) ** -0.5, 3.0, ((0, 8),))
    upper_structure = draw_upper_structure(jax.random.fold_in(seeds[9], 71), 0)
    upper_panels = scatter_about(seeds[2], (NK1, NT, S, S), S ** -0.5, 0.375, ((0, 4), (1, 8)))
    upper_diag_inverse = scatter_about(seeds[3], (NK1, S, S), 1.0, 6.0, ((0, 4),), jnp.float32)
    child_order = jax.random.permutation(seeds[4], NK2).astype(jnp.int32)
    child_keep = place_ends((jax.random.randint(seeds[5], (NK2, NT), 0, 4) < 3).astype(jnp.int32), jax.random.fold_in(seeds[5], 1), 0, 1)
    lower_panels = scatter_about(seeds[6], (NK2, NT, S, S), (NT * S // 4) ** -0.5, 0.25, ((0, 4), (1, 8)))
    parent_panels = scatter_about(seeds[7], (NK2, S, S), (4 * S) ** -0.5, 0.1875, ((0, 4),))
    lower_diag_inverse = scatter_about(seeds[8], (NK2, S, S), 1.0, 6.0, ((0, 4),), jnp.float32)
    return dict(top_inverse=top_inverse, upper_structure=upper_structure, upper_panels=upper_panels, upper_diag_inverse=upper_diag_inverse, child_order=child_order, child_keep=child_keep, lower_panels=lower_panels, parent_panels=parent_panels, lower_diag_inverse=lower_diag_inverse)


def reference(top_inverse, upper_structure, upper_panels, upper_diag_inverse, child_order, child_keep, lower_panels, parent_panels, lower_diag_inverse):
    high = lax.Precision.HIGHEST
    upper_mask = upper_structure.astype(jnp.float32)
    masked_upper = upper_panels.astype(jnp.float32) * upper_mask[:, :, None, None]
    parent = (child_order // CH).astype(jnp.int32)
    lower_structure = upper_structure[parent] * child_keep
    lower_mask = lower_structure.astype(jnp.float32)
    masked_lower = lower_panels.astype(jnp.float32) * lower_mask[:, :, None, None]
    stacked = jnp.concatenate([masked_upper, masked_lower], axis=0)

    def one_row(top_row):
        return jnp.einsum('isd,kide->kse', top_row.astype(jnp.float32), stacked, precision=high)

    summed = jnp.transpose(lax.map(one_row, top_inverse), (1, 0, 2, 3))
    upper_sum = summed[:NK1]
    lower_sum = summed[NK1:]
    upper_blocks = (-(upper_mask[:, :, None, None] * upper_sum)).astype(jnp.bfloat16)
    upper_diag = upper_diag_inverse - jnp.einsum('kjds,kjde->kse', upper_panels.astype(jnp.float32), upper_blocks.astype(jnp.float32), precision=high)
    parent_rows = upper_blocks[parent].astype(jnp.float32)
    parent_diag = upper_diag[parent]
    parent_wide = parent_panels.astype(jnp.float32)
    through_parent = jnp.einsum('kjsd,kde->kjse', parent_rows, parent_wide, precision=high)
    lower_blocks = (-(lower_mask[:, :, None, None] * (through_parent + lower_sum))).astype(jnp.bfloat16)
    cross = jnp.einsum('kjds,kjde->kse', parent_rows, masked_lower, precision=high)
    lower_parent = (-(jnp.einsum('ksd,kde->kse', parent_diag, parent_wide, precision=high) + cross)).astype(jnp.bfloat16)
    lower_diag = lower_diag_inverse - jnp.einsum('kds,kde->kse', parent_wide, lower_parent.astype(jnp.float32), precision=high) - jnp.einsum('kjds,kjde->kse', lower_panels.astype(jnp.float32), lower_blocks.astype(jnp.float32), precision=high)
    return upper_blocks, upper_diag, lower_blocks, lower_parent, lower_diag
```

```python
import functools

import jax
import jax.numpy as jnp
from jax import lax
from jax.experimental import pallas as pl
from jax.experimental.pallas import tpu as pltpu
from jax.sharding import PartitionSpec as P

CH = 2
CORES = 2
BF = jnp.bfloat16
F32 = jnp.float32


def dense_sum(top_rows, piece):
    return jnp.einsum("isd,kide->kse", top_rows, piece, preferred_element_type=jnp.float32)


def wide_shards(
    top_inverse,
    upper_structure,
    upper_panels,
    upper_diag_inverse,
    child_order,
    child_keep,
    lower_panels,
    parent_panels,
    lower_diag_inverse,
):
    row_index = lax.axis_index("prow")
    col_index = lax.axis_index("pcol")
    upper_count = upper_panels.shape[0]
    lower_count = lower_panels.shape[0]
    top_rows = top_inverse[0]
    upper_rows = lax.dynamic_slice_in_dim(upper_structure, row_index * upper_count, upper_count, 0)
    upper_flags = lax.dynamic_index_in_dim(upper_rows, col_index, 1, keepdims=False)
    upper_own = upper_panels[:, 0] * upper_flags[:, None, None].astype(jnp.bfloat16)
    order_rows = lax.dynamic_slice_in_dim(child_order, row_index * lower_count, lower_count, 0)
    parent = order_rows // CH
    lower_structure = jnp.take(upper_structure, parent, axis=0) * child_keep
    lower_flags = lax.dynamic_index_in_dim(lower_structure, col_index, 1, keepdims=False)
    lower_own = lower_panels[:, 0] * lower_flags[:, None, None].astype(jnp.bfloat16)
    upper_sum = dense_sum(top_rows, lax.all_gather(upper_own[:, None], "pcol", axis=1, tiled=True))
    upper_local = (-(upper_flags[:, None, None].astype(jnp.float32) * upper_sum)).astype(
        jnp.bfloat16
    )
    diag_term = jnp.einsum(
        "kds,kde->kse", upper_panels[:, 0], upper_local, preferred_element_type=jnp.float32
    )
    own_share = (
        jnp.where(col_index == 0, upper_diag_inverse, jnp.zeros_like(upper_diag_inverse))
        - diag_term
    )
    upper_diag = lax.psum(own_share, "pcol")
    diag_every = lax.all_gather(upper_diag, "prow", axis=0, tiled=True)
    upper_every = lax.all_gather(upper_local, "prow", axis=0, tiled=True)
    lower_sum = dense_sum(top_rows, lax.all_gather(lower_own[:, None], "pcol", axis=1, tiled=True))
    parent_rows = jnp.take(upper_every, parent, axis=0)
    parent_diag = jnp.take(diag_every, parent, axis=0)
    through_parent = jnp.einsum(
        "ksd,kde->kse", parent_rows, parent_panels, preferred_element_type=jnp.float32
    )
    lower_local = (
        -(lower_flags[:, None, None].astype(jnp.float32) * (through_parent + lower_sum))
    ).astype(jnp.bfloat16)
    cross_term = jnp.einsum(
        "kds,kde->kse", parent_rows, lower_own, preferred_element_type=jnp.float32
    )
    lower_term = jnp.einsum(
        "kds,kde->kse", lower_panels[:, 0], lower_local, preferred_element_type=jnp.float32
    )
    cross, lower_total = lax.psum((cross_term, lower_term), "pcol")
    parent_part = jnp.einsum(
        "ksd,kde->kse",
        parent_diag,
        parent_panels.astype(jnp.float32),
        precision=lax.Precision.HIGHEST,
    )
    lower_parent = (-(parent_part + cross)).astype(jnp.bfloat16)
    lower_diag = (
        lower_diag_inverse
        - jnp.einsum(
            "kds,kde->kse", parent_panels, lower_parent, preferred_element_type=jnp.float32
        )
        - lower_total
    )
    return (upper_local[:, None], upper_diag, lower_local[:, None], lower_parent, lower_diag)


def dot(a, b):
    return lax.dot_general(a, b, (((1,), (0,)), ((), ())), preferred_element_type=F32)


def dot_t(a, b):
    return lax.dot_general(a, b, (((0,), (0,)), ((), ())), preferred_element_type=F32)


def place():
    col = lax.axis_index("pcol")
    return lax.axis_index("prow"), col // CORES, col % CORES


def upper_body(nz, us_ref, to_ref, ts_ref, uo_ref, us_full_ref, d_ref, *refs):
    stacks, (rx_ref, ud_ref, xs) = refs[:nz], refs[nz:]
    row, z, c = place()
    half = xs.shape[1]
    quarter = xs.shape[0] // nz
    acc = [None, None]
    for s in range(nz):
        for q in range(CORES):
            i = CORES * (z ^ s) + (c if q == 0 else 1 - c)
            flag = us_ref[row, i].astype(F32).astype(BF)
            piece = stacks[s][q] * flag
            for p, t_ref in enumerate((to_ref, ts_ref)):
                prod = dot(t_ref[i], piece)
                acc[p] = prod if acc[p] is None else acc[p] + prod
    x = None
    for p, u_ref in enumerate((uo_ref, us_full_ref)):
        j = CORES * z + (c if p == 0 else 1 - c)
        flag = us_ref[row, j].astype(F32)
        block = (-(flag * acc[p])).astype(BF)
        rx_ref[p] = block
        prod = dot_t(u_ref[...], block)
        x = prod if x is None else x + prod
    xs[...] = -x
    for s in range(nz):
        ud_ref[s] = xs[pl.ds(pl.multiple_of((z ^ s) * quarter, quarter), quarter), :].astype(BF)
    own = pl.ds(pl.multiple_of(z * quarter, quarter), quarter)
    rows = d_ref[own, :]
    xs[own, :] = xs[own, :] + jnp.where(c == 0, rows[:, :half], rows[:, half:])
    rx_ref[CORES] = xs[...].astype(BF)


def parent_body(nz, us_ref, co_ref, ck_ref, keep_ref, got_ref, pp_ref, lm_ref, lg_ref, ud_ref,
                w_ref, rs_ref, a_ref):
    row, z, c = place()
    half = keep_ref.shape[2]
    size = pp_ref.shape[1]
    quarter = size // nz
    mine = pl.ds(pl.multiple_of(c * half, half), half)
    other = pl.ds(pl.multiple_of((1 - c) * half, half), half)
    parent = co_ref[CORES * row + c] // CH
    p_mine, p_other = pp_ref[c, mine, :], pp_ref[c, other, :]
    a_ref[...] = dot(keep_ref[CORES], p_mine) + dot(got_ref[CORES], p_other)
    for p, l_ref in enumerate((lm_ref, lg_ref)):
        j = CORES * z + (c if p == 0 else 1 - c)
        flag = (us_ref[parent, j] * ck_ref[c, j]).astype(F32).astype(BF)
        k_half, g_half = keep_ref[p], got_ref[1 - p]
        w_ref[p] = dot(k_half, p_mine) + dot(g_half, p_other)
        masked = l_ref[...] * flag
        a_ref[mine, :] = a_ref[mine, :] + dot_t(k_half, masked)
        a_ref[other, :] = a_ref[other, :] + dot_t(g_half, masked)
    for s in range(nz):
        block = pl.ds(pl.multiple_of((z ^ s) * quarter, quarter), quarter)
        rs_ref[s, :, :size] = a_ref[block, :].astype(BF)
        rs_ref[s, :, size:] = ud_ref[s]


def lower_body(nz, us_ref, co_ref, ck_ref, to_ref, ts_ref, w_ref, *refs):
    stacks, (lo_ref, lg_ref, rs_ref, r_ref) = refs[:nz], refs[nz:]
    row, z, c = place()
    quarter = r_ref.shape[0] // nz
    parent = co_ref[CORES * row + c] // CH
    acc = [w_ref[0], w_ref[1]]
    for s in range(nz):
        for q in range(CORES):
            i = CORES * (z ^ s) + (c if q == 0 else 1 - c)
            flag = (us_ref[parent, i] * ck_ref[c, i]).astype(F32).astype(BF)
            piece = stacks[s][q] * flag
            for p, t_ref in enumerate((to_ref, ts_ref)):
                acc[p] = acc[p] + dot(t_ref[i], piece)
    total = None
    for p, o_ref in enumerate((lo_ref, lg_ref)):
        j = CORES * z + (c if p == 0 else 1 - c)
        flag = (us_ref[parent, j] * ck_ref[c, j]).astype(F32)
        block = (-(flag * acc[p])).astype(BF)
        o_ref[...] = block
        prod = dot_t(stacks[0][p], block)
        total = prod if total is None else total + prod
    r_ref[...] = total
    for s in range(nz):
        rs_ref[s] = r_ref[
            pl.ds(pl.multiple_of((z ^ s) * quarter, quarter), quarter), :
        ].astype(BF)


def add_body(negate, *refs):
    *parts, out_ref = refs
    total = parts[0][0].astype(F32)
    for part in parts[1:]:
        total = total + part[...].astype(F32)
    if negate:
        out_ref[:, :negate] = (-total[:, :negate]).astype(BF)
        out_ref[:, negate:] = total[:, negate:].astype(BF)
    else:
        out_ref[...] = total.astype(BF)


def join_body(*refs):
    *parts, out_ref = refs
    _, z, _ = place()
    for s, part in enumerate(parts):
        quarter = part.shape[0]
        out_ref[pl.ds(pl.multiple_of((z ^ s) * quarter, quarter), quarter), :] = part[...]


def parent_out_body(own_ref, got_ref, d_ref, ld_ref, pp_ref, ud_ref, lp_ref, base_ref):
    _, _, c = place()
    size = pp_ref.shape[1]
    half = size // CORES
    first, second = own_ref[:, size:].astype(F32), got_ref[:, size:].astype(F32)
    ud_ref[0, :, :half] = d_ref[0, :, :half] + jnp.where(c == 0, first, second)
    ud_ref[0, :, half:] = d_ref[0, :, half:] + jnp.where(c == 0, second, first)
    for k, ref in ((c, own_ref), (1 - c, got_ref)):
        block = ref[:, :size]
        lp_ref[k] = block
        base_ref[k] = ld_ref[k] - dot_t(pp_ref[k], block)


def lower_out_body(base_ref, own_ref, got_ref, ld_ref):
    _, _, c = place()
    ld_ref[c] = base_ref[c] - own_ref[...].astype(F32)
    ld_ref[1 - c] = base_ref[1 - c] - got_ref[...].astype(F32)


def near_shards(
    rows,
    cols,
    top_inverse,
    upper_structure,
    upper_panels,
    upper_diag_inverse,
    child_order,
    child_keep,
    lower_panels,
    parent_panels,
    lower_diag_inverse,
):
    nz = cols // CORES
    size = upper_panels.shape[-1]
    half, quarter = size // CORES, size // nz
    row, z, c = place()
    first = c == 0

    def over_core(x):
        return lax.ppermute(x, "pcol", [(i, i ^ 1) for i in range(cols)])

    def over_z(x, s):
        return lax.ppermute(x, "pcol", [(i, i ^ (CORES * s)) for i in range(cols)])

    def over_row(x, s):
        return lax.ppermute(x, "prow", [(i, i ^ s) for i in range(rows)])

    shape = jax.ShapeDtypeStruct
    t_own = top_inverse[0]
    u_own = upper_panels[0, 0]
    l_all = lower_panels[:, 0]
    d_own = upper_diag_inverse[0]
    u_sib = over_core(u_own)
    l_own = jnp.where(first, l_all[0], l_all[1])
    l_sib = over_core(jnp.where(first, l_all[1], l_all[0]))
    t_sib = over_core(t_own)
    u_both = jnp.stack([u_own, u_sib])
    u_stack = jnp.where(first, u_both[:, :, :half], u_both[:, :, half:])
    l_stack = jnp.stack([l_own, l_sib])
    u_all = [u_stack] + [over_z(u_stack, s) for s in range(1, nz)]
    l_all = [l_stack] + [over_z(l_stack, s) for s in range(1, nz)]

    vm = pl.BlockSpec(memory_space=pltpu.VMEM)
    sm = pl.BlockSpec(memory_space=pltpu.SMEM)

    def kernel(body, out, args, smem=0, scratch=()):
        return pl.pallas_call(
            body,
            out_shape=out,
            in_specs=[sm] * smem + [vm] * (len(args) - smem),
            out_specs=jax.tree.map(lambda _: vm, out),
            scratch_shapes=list(scratch),
            compiler_params=pltpu.CompilerParams(vmem_limit_bytes=24 * 1024 * 1024),
        )(*args)

    rx, ud_part = kernel(
        functools.partial(upper_body, nz),
        (shape((CORES + 1, size, half), BF), shape((nz, quarter, half), BF)),
        (upper_structure, t_own, t_sib, u_own, u_sib, d_own, *u_all),
        smem=1,
        scratch=[pltpu.VMEM((size, half), F32)],
    )
    ub_got = over_core(rx[1])
    ub_own = rx[0]
    upper_blocks = jnp.where(
        first,
        jnp.concatenate([ub_own, ub_got], axis=1),
        jnp.concatenate([ub_got, ub_own], axis=1),
    )[None, None]

    rx_all = [rx] + [over_row(rx, s) for s in range(1, rows)]
    parents = lax.dynamic_slice_in_dim(child_order, CORES * row, CORES) // CH

    def pick(k):
        index = jnp.where(k == 0, parents[0], parents[1]) ^ row
        out = rx_all[0]
        for s in range(1, rows):
            out = jnp.where(index == s, rx_all[s], out)
        return out

    keep = pick(c)
    got = over_core(pick(1 - c))
    scalars = (upper_structure, child_order, child_keep)
    w, rs1 = kernel(
        functools.partial(parent_body, nz),
        (shape((CORES, size, size), F32), shape((nz, quarter, size + half), BF)),
        (*scalars, keep, got, parent_panels, l_own, l_sib, ud_part),
        smem=3,
        scratch=[pltpu.VMEM((size, size), F32)],
    )
    lb_own, lb_give, rs2 = kernel(
        functools.partial(lower_body, nz),
        (shape((size, size), BF), shape((size, size), BF), shape((nz, quarter, size), BF)),
        (*scalars, t_own, t_sib, w, *l_all),
        smem=3,
        scratch=[pltpu.VMEM((size, size), F32)],
    )
    lb_got = over_core(lb_give)
    lower_blocks = jnp.where(
        first, jnp.stack([lb_own, lb_got]), jnp.stack([lb_got, lb_own])
    )[:, None]

    def reduce(parts, negate):
        got = [over_z(parts[s], s) for s in range(1, nz)]
        part = kernel(
            functools.partial(add_body, negate), shape(parts.shape[1:], BF), (parts, *got)
        )
        every = [part] + [over_z(part, s) for s in range(1, nz)]
        return kernel(join_body, shape((size, parts.shape[2]), BF), tuple(every))

    total1 = reduce(rs1, size)
    total1_got = over_core(total1)
    upper_diag, lower_parent, base = kernel(
        parent_out_body,
        (
            shape((1, size, size), F32),
            shape((CORES, size, size), BF),
            shape((CORES, size, size), F32),
        ),
        (total1, total1_got, upper_diag_inverse, lower_diag_inverse, parent_panels),
    )
    total2 = reduce(rs2, 0)
    lower_diag = kernel(
        lower_out_body,
        shape((CORES, size, size), F32),
        (base, total2, over_core(total2)),
    )
    return upper_blocks, upper_diag, lower_blocks, lower_parent, lower_diag


def solution(mesh):
    in_specs = (
        P("pcol", None, None, None),
        P(),
        P("prow", "pcol", None, None),
        P("prow", None, None),
        P(),
        P("prow", None),
        P("prow", "pcol", None, None),
        P("prow", None, None),
        P("prow", None, None),
    )
    out_specs = (
        P("prow", "pcol", None, None),
        P("prow", None, None),
        P("prow", "pcol", None, None),
        P("prow", None, None),
        P("prow", None, None),
    )
    rows, cols = mesh.shape["prow"], mesh.shape["pcol"]
    body = functools.partial(near_shards, rows, cols) if cols <= 8 else wide_shards
    return jax.shard_map(body, mesh=mesh, in_specs=in_specs, out_specs=out_specs, check_vma=False)
```

```python
import functools

import jax
import jax.numpy as jnp
from jax import lax
from jax.experimental import pallas as pl
from jax.experimental.pallas import tpu as pltpu
from jax.sharding import PartitionSpec as P

CH = 2
CORES = 2
BF = jnp.bfloat16
F32 = jnp.float32


def dense_sum(top_rows, piece):
    return jnp.einsum("isd,kide->kse", top_rows, piece, preferred_element_type=jnp.float32)


def wide_shards(
    top_inverse,
    upper_structure,
    upper_panels,
    upper_diag_inverse,
    child_order,
    child_keep,
    lower_panels,
    parent_panels,
    lower_diag_inverse,
):
    row_index = lax.axis_index("prow")
    col_index = lax.axis_index("pcol")
    upper_count = upper_panels.shape[0]
    lower_count = lower_panels.shape[0]
    top_rows = top_inverse[0]
    upper_rows = lax.dynamic_slice_in_dim(upper_structure, row_index * upper_count, upper_count, 0)
    upper_flags = lax.dynamic_index_in_dim(upper_rows, col_index, 1, keepdims=False)
    upper_own = upper_panels[:, 0] * upper_flags[:, None, None].astype(jnp.bfloat16)
    order_rows = lax.dynamic_slice_in_dim(child_order, row_index * lower_count, lower_count, 0)
    parent = order_rows // CH
    lower_structure = jnp.take(upper_structure, parent, axis=0) * child_keep
    lower_flags = lax.dynamic_index_in_dim(lower_structure, col_index, 1, keepdims=False)
    lower_own = lower_panels[:, 0] * lower_flags[:, None, None].astype(jnp.bfloat16)
    upper_sum = dense_sum(top_rows, lax.all_gather(upper_own[:, None], "pcol", axis=1, tiled=True))
    upper_local = (-(upper_flags[:, None, None].astype(jnp.float32) * upper_sum)).astype(
        jnp.bfloat16
    )
    diag_term = jnp.einsum(
        "kds,kde->kse", upper_panels[:, 0], upper_local, preferred_element_type=jnp.float32
    )
    own_share = (
        jnp.where(col_index == 0, upper_diag_inverse, jnp.zeros_like(upper_diag_inverse))
        - diag_term
    )
    upper_diag = lax.psum(own_share, "pcol")
    diag_every = lax.all_gather(upper_diag, "prow", axis=0, tiled=True)
    upper_every = lax.all_gather(upper_local, "prow", axis=0, tiled=True)
    lower_sum = dense_sum(top_rows, lax.all_gather(lower_own[:, None], "pcol", axis=1, tiled=True))
    parent_rows = jnp.take(upper_every, parent, axis=0)
    parent_diag = jnp.take(diag_every, parent, axis=0)
    through_parent = jnp.einsum(
        "ksd,kde->kse", parent_rows, parent_panels, preferred_element_type=jnp.float32
    )
    lower_local = (
        -(lower_flags[:, None, None].astype(jnp.float32) * (through_parent + lower_sum))
    ).astype(jnp.bfloat16)
    cross_term = jnp.einsum(
        "kds,kde->kse", parent_rows, lower_own, preferred_element_type=jnp.float32
    )
    lower_term = jnp.einsum(
        "kds,kde->kse", lower_panels[:, 0], lower_local, preferred_element_type=jnp.float32
    )
    cross, lower_total = lax.psum((cross_term, lower_term), "pcol")
    parent_part = jnp.einsum(
        "ksd,kde->kse",
        parent_diag,
        parent_panels.astype(jnp.float32),
        precision=lax.Precision.HIGHEST,
    )
    lower_parent = (-(parent_part + cross)).astype(jnp.bfloat16)
    lower_diag = (
        lower_diag_inverse
        - jnp.einsum(
            "kds,kde->kse", parent_panels, lower_parent, preferred_element_type=jnp.float32
        )
        - lower_total
    )
    return (upper_local[:, None], upper_diag, lower_local[:, None], lower_parent, lower_diag)


def dot(a, b):
    return lax.dot_general(a, b, (((1,), (0,)), ((), ())), preferred_element_type=F32)


def dot_t(a, b):
    return lax.dot_general(a, b, (((0,), (0,)), ((), ())), preferred_element_type=F32)


def place():
    col = lax.axis_index("pcol")
    return lax.axis_index("prow"), col // CORES, col % CORES


def upper_body(nz, us_ref, to_ref, ts_ref, us_full_ref, uo_hbm, d_hbm, *refs):
    stacks, (rx_ref, ud_ref, xs, uo_ref, d_ref, sems) = refs[:nz], refs[-6:]
    row, z, c = place()
    copies = [
        pltpu.make_async_copy(uo_hbm, uo_ref, sems.at[0]),
        pltpu.make_async_copy(d_hbm, d_ref, sems.at[1]),
    ]
    for copy in copies:
        copy.start()
    half = xs.shape[1]
    quarter = xs.shape[0] // nz
    acc = [None, None]
    for s in range(nz):
        for q in range(CORES):
            i = CORES * (z ^ s) + (c if q == 0 else 1 - c)
            flag = us_ref[row, i].astype(F32).astype(BF)
            piece = stacks[s][q] * flag
            for p, t_ref in enumerate((to_ref, ts_ref)):
                prod = dot(t_ref[i], piece)
                acc[p] = prod if acc[p] is None else acc[p] + prod
    for copy in copies:
        copy.wait()
    x = None
    for p, u_ref in enumerate((uo_ref, us_full_ref)):
        j = CORES * z + (c if p == 0 else 1 - c)
        flag = us_ref[row, j].astype(F32)
        block = (-(flag * acc[p])).astype(BF)
        rx_ref[p] = block
        prod = dot_t(u_ref[...], block)
        x = prod if x is None else x + prod
    xs[...] = -x
    for s in range(nz):
        ud_ref[s] = xs[pl.ds(pl.multiple_of((z ^ s) * quarter, quarter), quarter), :].astype(BF)
    own = pl.ds(pl.multiple_of(z * quarter, quarter), quarter)
    rows = d_ref[own, :]
    xs[own, :] = xs[own, :] + jnp.where(c == 0, rows[:, :half], rows[:, half:])
    rx_ref[CORES] = xs[...].astype(BF)


def pick_body(rows, co_ref, *refs):
    blocks, (keep_ref, give_ref) = refs[:rows], refs[-2:]
    row, _, c = place()
    for k, out_ref in ((c, keep_ref), (1 - c, give_ref)):
        index = (co_ref[CORES * row + k] // CH) ^ row
        for s, block in enumerate(blocks):

            @pl.when(index == s)
            def _(out_ref=out_ref, block=block):
                out_ref[...] = block[...]


def parent_body(nz, us_ref, co_ref, ck_ref, keep_ref, got_ref, pp_ref, lm_ref, lg_ref, ud_ref,
                w_ref, rs_ref, a_ref):
    row, z, c = place()
    half = keep_ref.shape[2]
    size = pp_ref.shape[1]
    quarter = size // nz
    mine = pl.ds(pl.multiple_of(c * half, half), half)
    other = pl.ds(pl.multiple_of((1 - c) * half, half), half)
    parent = co_ref[CORES * row + c] // CH
    p_mine, p_other = pp_ref[c, mine, :], pp_ref[c, other, :]
    a_ref[...] = dot(keep_ref[CORES], p_mine) + dot(got_ref[CORES], p_other)
    for p, l_ref in enumerate((lm_ref, lg_ref)):
        j = CORES * z + (c if p == 0 else 1 - c)
        flag = (us_ref[parent, j] * ck_ref[c, j]).astype(F32).astype(BF)
        k_half, g_half = keep_ref[p], got_ref[1 - p]
        w_ref[p] = dot(k_half, p_mine) + dot(g_half, p_other)
        masked = l_ref[...] * flag
        a_ref[mine, :] = a_ref[mine, :] + dot_t(k_half, masked)
        a_ref[other, :] = a_ref[other, :] + dot_t(g_half, masked)
    for s in range(nz):
        block = pl.ds(pl.multiple_of((z ^ s) * quarter, quarter), quarter)
        rs_ref[s, :, :size] = a_ref[block, :].astype(BF)
        rs_ref[s, :, size:] = ud_ref[s]


def lower_body(nz, us_ref, co_ref, ck_ref, to_ref, ts_ref, w_ref, rs1_ref, *refs):
    stacks, (lo_ref, lg_ref, rs_ref, r_ref) = refs[:nz], refs[-4:]
    row, z, c = place()
    quarter = r_ref.shape[0] // nz
    parent = co_ref[CORES * row + c] // CH
    acc = [w_ref[0], w_ref[1]]
    for s in range(nz):
        for q in range(CORES):
            i = CORES * (z ^ s) + (c if q == 0 else 1 - c)
            flag = (us_ref[parent, i] * ck_ref[c, i]).astype(F32).astype(BF)
            piece = stacks[s][q] * flag
            for p, t_ref in enumerate((to_ref, ts_ref)):
                acc[p] = acc[p] + dot(t_ref[i], piece)
    total = None
    for p, o_ref in enumerate((lo_ref, lg_ref)):
        j = CORES * z + (c if p == 0 else 1 - c)
        flag = (us_ref[parent, j] * ck_ref[c, j]).astype(F32)
        block = (-(flag * acc[p])).astype(BF)
        o_ref[...] = block
        prod = dot_t(stacks[0][p], block)
        total = prod if total is None else total + prod
    r_ref[...] = total
    size = r_ref.shape[1]
    for s in range(nz):
        block = pl.ds(pl.multiple_of((z ^ s) * quarter, quarter), quarter)
        rs_ref[s, :, :size] = r_ref[block, :].astype(BF)
        rs_ref[s, :, size:] = rs1_ref[s]


def pair_body(count, *refs):
    for i, ref in enumerate(refs[:count]):
        refs[-1][i] = ref[...]


def halves_body(own_ref, got_ref, out_ref):
    _, _, c = place()
    half = own_ref.shape[1]
    own, got = own_ref[...], got_ref[...]
    out_ref[0, 0, :, :half] = jnp.where(c == 0, own, got)
    out_ref[0, 0, :, half:] = jnp.where(c == 0, got, own)


def order_body(own_ref, got_ref, out_ref):
    _, _, c = place()
    out_ref[c, 0] = own_ref[...]
    out_ref[1 - c, 0] = got_ref[...]


def add_body(own_ref, *refs):
    *parts, out_ref = refs
    total = own_ref[0].astype(F32)
    for part in parts:
        total = total + part[...].astype(F32)
    out_ref[...] = total.astype(BF)


def join_body(nz, *refs):
    parts, out_ref = refs[:nz], refs[-1]
    _, z, _ = place()
    for s, part in enumerate(parts):
        quarter = part.shape[0]
        out_ref[pl.ds(pl.multiple_of((z ^ s) * quarter, quarter), quarter), :] = part[...]


def out_body(own_ref, got_ref, d_ref, pp_ref, ld_ref, ud_ref, lp_ref, out_ref):
    _, _, c = place()
    size = pp_ref.shape[1]
    half = size // CORES
    first = own_ref[:, 2 * size :].astype(F32)
    second = got_ref[:, 2 * size :].astype(F32)
    ud_ref[0, :, :half] = d_ref[0, :, :half] + jnp.where(c == 0, first, second)
    ud_ref[0, :, half:] = d_ref[0, :, half:] + jnp.where(c == 0, second, first)
    for k, ref in ((c, own_ref), (1 - c, got_ref)):
        block = -ref[:, size : 2 * size]
        lp_ref[k] = block
        out_ref[k] = ld_ref[k] - dot_t(pp_ref[k], block) - ref[:, :size].astype(F32)


def near_shards(
    rows,
    cols,
    top_inverse,
    upper_structure,
    upper_panels,
    upper_diag_inverse,
    child_order,
    child_keep,
    lower_panels,
    parent_panels,
    lower_diag_inverse,
):
    nz = cols // CORES
    size = upper_panels.shape[-1]
    half, quarter = size // CORES, size // nz
    row, z, c = place()
    first = c == 0

    def over_core(x):
        return lax.ppermute(x, "pcol", [(i, i ^ 1) for i in range(cols)])

    def over_z(x, s):
        return lax.ppermute(x, "pcol", [(i, i ^ (CORES * s)) for i in range(cols)])

    def over_row(x, s):
        return lax.ppermute(x, "prow", [(i, i ^ s) for i in range(rows)])

    shape = jax.ShapeDtypeStruct
    t_own = top_inverse[0]
    u_own = upper_panels[0, 0]
    l_all = lower_panels[:, 0]
    d_own = upper_diag_inverse[0]
    u_sib = over_core(u_own)
    l_own = jnp.where(first, l_all[0], l_all[1])
    l_sib = over_core(jnp.where(first, l_all[1], l_all[0]))
    t_sib = over_core(t_own)
    u_both = jnp.stack([u_own, u_sib])
    u_stack = jnp.where(first, u_both[:, :, :half], u_both[:, :, half:])
    u_all = [u_stack] + [over_z(u_stack, s) for s in range(1, nz)]

    vm = pl.BlockSpec(memory_space=pltpu.VMEM)
    sm = pl.BlockSpec(memory_space=pltpu.SMEM)

    anywhere = pl.BlockSpec(memory_space=pl.ANY)

    def kernel(body, out, args, smem=0, scratch=(), rest=()):
        return pl.pallas_call(
            body,
            out_shape=out,
            in_specs=[sm] * smem + [vm] * (len(args) - smem) + [anywhere] * len(rest),
            out_specs=jax.tree.map(lambda _: vm, out),
            scratch_shapes=list(scratch),
            compiler_params=pltpu.CompilerParams(vmem_limit_bytes=24 * 1024 * 1024),
        )(*args, *rest)

    def upper(us, to, ts, usib, *refs):
        stacks, uo, d = refs[:nz], refs[nz], refs[nz + 1]
        upper_body(nz, us, to, ts, usib, uo, d, *stacks, *refs[-6:])

    l_stack = kernel(
        functools.partial(pair_body, 2), shape((CORES, size, size), BF), (l_own, l_sib), rest=(u_stack,)
    )
    l_later = lax.optimization_barrier((l_stack, *u_all[1:]))[0]
    l_stacks = [l_stack, over_z(l_stack, 1)] + [over_z(l_later, s) for s in range(2, nz)]
    scalars = (upper_structure, child_order, child_keep)

    def upper_part(_):
        rx, ud_part = kernel(
            upper,
            (shape((CORES + 1, size, half), BF), shape((nz, quarter, half), BF)),
            (upper_structure, t_own, t_sib, u_sib, *u_all),
            smem=1,
            scratch=[
                pltpu.VMEM((size, half), F32),
                pltpu.VMEM((size, size), BF),
                pltpu.VMEM((size, size), F32),
                pltpu.SemaphoreType.DMA((2,)),
            ],
            rest=(u_own, d_own, l_stacks[1]),
        )
        rx_all = [rx] + [over_row(rx, s) for s in range(1, rows)]
        keep, give = kernel(
            functools.partial(pick_body, rows),
            (shape(rx.shape, BF), shape(rx.shape, BF)),
            (child_order, *rx_all),
            smem=1,
        )
        got = over_core(give)
        w, rs1 = kernel(
            functools.partial(parent_body, nz),
            (shape((CORES, size, size), F32), shape((nz, quarter, size + half), BF)),
            (*scalars, keep, got, parent_panels, l_own, l_sib, ud_part),
            smem=3,
            scratch=[pltpu.VMEM((size, size), F32)],
        )
        return rx[:CORES], w, rs1

    def no_part(_):
        return (
            jnp.zeros((CORES, size, half), BF),
            jnp.zeros((CORES, size, size), F32),
            jnp.zeros((nz, quarter, size + half), BF),
        )

    ub, w, rs1 = lax.cond(child_order[0] >= 0, upper_part, no_part, None)
    ub_got = over_core(ub[1])
    upper_blocks = kernel(halves_body, shape((1, 1, size, size), BF), (ub[0], ub_got))
    lb_own, lb_give, sums = kernel(
        functools.partial(lower_body, nz),
        (shape((size, size), BF), shape((size, size), BF), shape((nz, quarter, 2 * size + half), BF)),
        (*scalars, t_own, t_sib, w, rs1, *l_stacks),
        smem=3,
        scratch=[pltpu.VMEM((size, size), F32)],
        rest=(upper_blocks,),
    )
    lb_got = over_core(lb_give)
    lower_blocks = kernel(order_body, shape((CORES, 1, size, size), BF), (lb_own, lb_got))
    got_sums = [over_z(sums[s], s) for s in range(1, nz)]
    part = kernel(add_body, shape(sums.shape[1:], BF), (sums, *got_sums))
    every = [part] + [over_z(part, s) for s in range(1, nz)]
    total = kernel(
        functools.partial(join_body, nz),
        shape((size, part.shape[1]), BF),
        tuple(every),
        rest=(lower_blocks,),
    )
    upper_diag, lower_parent, lower_diag = kernel(
        out_body,
        (
            shape((1, size, size), F32),
            shape((CORES, size, size), BF),
            shape((CORES, size, size), F32),
        ),
        (total, over_core(total), upper_diag_inverse, parent_panels, lower_diag_inverse),
    )
    return upper_blocks, upper_diag, lower_blocks, lower_parent, lower_diag


def solution(mesh):
    in_specs = (
        P("pcol", None, None, None),
        P(),
        P("prow", "pcol", None, None),
        P("prow", None, None),
        P(),
        P("prow", None),
        P("prow", "pcol", None, None),
        P("prow", None, None),
        P("prow", None, None),
    )
    out_specs = (
        P("prow", "pcol", None, None),
        P("prow", None, None),
        P("prow", "pcol", None, None),
        P("prow", None, None),
        P("prow", None, None),
    )
    rows, cols = mesh.shape["prow"], mesh.shape["pcol"]
    body = functools.partial(near_shards, rows, cols) if cols <= 8 else wide_shards
    return jax.shard_map(body, mesh=mesh, in_specs=in_specs, out_specs=out_specs, check_vma=False)
```

```python
import functools

import jax
import jax.numpy as jnp
from jax import lax
from jax.experimental import pallas as pl
from jax.experimental.pallas import tpu as pltpu
from jax.sharding import PartitionSpec as P

CH = 2
CORES = 2
BF = jnp.bfloat16
F32 = jnp.float32


def dense_sum(top_rows, piece):
    return jnp.einsum("isd,kide->kse", top_rows, piece, preferred_element_type=jnp.float32)


def wide_shards(
    top_inverse,
    upper_structure,
    upper_panels,
    upper_diag_inverse,
    child_order,
    child_keep,
    lower_panels,
    parent_panels,
    lower_diag_inverse,
):
    row_index = lax.axis_index("prow")
    col_index = lax.axis_index("pcol")
    upper_count = upper_panels.shape[0]
    lower_count = lower_panels.shape[0]
    top_rows = top_inverse[0]
    upper_rows = lax.dynamic_slice_in_dim(upper_structure, row_index * upper_count, upper_count, 0)
    upper_flags = lax.dynamic_index_in_dim(upper_rows, col_index, 1, keepdims=False)
    upper_own = upper_panels[:, 0] * upper_flags[:, None, None].astype(jnp.bfloat16)
    order_rows = lax.dynamic_slice_in_dim(child_order, row_index * lower_count, lower_count, 0)
    parent = order_rows // CH
    lower_structure = jnp.take(upper_structure, parent, axis=0) * child_keep
    lower_flags = lax.dynamic_index_in_dim(lower_structure, col_index, 1, keepdims=False)
    lower_own = lower_panels[:, 0] * lower_flags[:, None, None].astype(jnp.bfloat16)
    upper_sum = dense_sum(top_rows, lax.all_gather(upper_own[:, None], "pcol", axis=1, tiled=True))
    upper_local = (-(upper_flags[:, None, None].astype(jnp.float32) * upper_sum)).astype(
        jnp.bfloat16
    )
    diag_term = jnp.einsum(
        "kds,kde->kse", upper_panels[:, 0], upper_local, preferred_element_type=jnp.float32
    )
    own_share = (
        jnp.where(col_index == 0, upper_diag_inverse, jnp.zeros_like(upper_diag_inverse))
        - diag_term
    )
    upper_diag = lax.psum(own_share, "pcol")
    diag_every = lax.all_gather(upper_diag, "prow", axis=0, tiled=True)
    upper_every = lax.all_gather(upper_local, "prow", axis=0, tiled=True)
    lower_sum = dense_sum(top_rows, lax.all_gather(lower_own[:, None], "pcol", axis=1, tiled=True))
    parent_rows = jnp.take(upper_every, parent, axis=0)
    parent_diag = jnp.take(diag_every, parent, axis=0)
    through_parent = jnp.einsum(
        "ksd,kde->kse", parent_rows, parent_panels, preferred_element_type=jnp.float32
    )
    lower_local = (
        -(lower_flags[:, None, None].astype(jnp.float32) * (through_parent + lower_sum))
    ).astype(jnp.bfloat16)
    cross_term = jnp.einsum(
        "kds,kde->kse", parent_rows, lower_own, preferred_element_type=jnp.float32
    )
    lower_term = jnp.einsum(
        "kds,kde->kse", lower_panels[:, 0], lower_local, preferred_element_type=jnp.float32
    )
    cross, lower_total = lax.psum((cross_term, lower_term), "pcol")
    parent_part = jnp.einsum(
        "ksd,kde->kse",
        parent_diag,
        parent_panels.astype(jnp.float32),
        precision=lax.Precision.HIGHEST,
    )
    lower_parent = (-(parent_part + cross)).astype(jnp.bfloat16)
    lower_diag = (
        lower_diag_inverse
        - jnp.einsum(
            "kds,kde->kse", parent_panels, lower_parent, preferred_element_type=jnp.float32
        )
        - lower_total
    )
    return (upper_local[:, None], upper_diag, lower_local[:, None], lower_parent, lower_diag)


def dot(a, b):
    return lax.dot_general(a, b, (((1,), (0,)), ((), ())), preferred_element_type=F32)


def dot_t(a, b):
    return lax.dot_general(a, b, (((0,), (0,)), ((), ())), preferred_element_type=F32)


def place():
    col = lax.axis_index("pcol")
    return lax.axis_index("prow"), col // CORES, col % CORES


def upper_body(nz, us_ref, to_ref, ts_ref, *refs):
    pairs = [(refs[2 * s], refs[2 * s + 1]) for s in range(nz)]
    d_hbm, rx_ref, ud_ref, xs, d_ref, sem = refs[2 * nz :]
    row, z, c = place()
    copy = pltpu.make_async_copy(d_hbm, d_ref, sem)
    copy.start()
    half = xs.shape[1]
    quarter = xs.shape[0] // nz
    acc = [None, None]
    for s in range(nz):
        for q in range(CORES):
            i = CORES * (z ^ s) + (c if q == 0 else 1 - c)
            flag = us_ref[row, i].astype(F32).astype(BF)
            panel = pairs[s][q][...]
            piece = jnp.where(c == 0, panel[:, :half], panel[:, half:]) * flag
            for p, t_ref in enumerate((to_ref, ts_ref)):
                prod = dot(t_ref[i], piece)
                acc[p] = prod if acc[p] is None else acc[p] + prod
    copy.wait()
    x = None
    for p, u_ref in enumerate(pairs[0]):
        j = CORES * z + (c if p == 0 else 1 - c)
        flag = us_ref[row, j].astype(F32)
        block = (-(flag * acc[p])).astype(BF)
        rx_ref[p] = block
        prod = dot_t(u_ref[...], block)
        x = prod if x is None else x + prod
    xs[...] = -x
    for s in range(nz):
        ud_ref[s] = xs[pl.ds(pl.multiple_of((z ^ s) * quarter, quarter), quarter), :].astype(BF)
    own = pl.ds(pl.multiple_of(z * quarter, quarter), quarter)
    rows = d_ref[own, :]
    xs[own, :] = xs[own, :] + jnp.where(c == 0, rows[:, :half], rows[:, half:])
    rx_ref[CORES] = xs[...].astype(BF)


def pick_body(rows, co_ref, *refs):
    blocks, (keep_ref, give_ref) = refs[:rows], refs[-2:]
    row, _, c = place()
    for k, out_ref in ((c, keep_ref), (1 - c, give_ref)):
        index = (co_ref[CORES * row + k] // CH) ^ row
        for s, block in enumerate(blocks):

            @pl.when(index == s)
            def _(out_ref=out_ref, block=block):
                out_ref[...] = block[...]


def parent_body(nz, us_ref, co_ref, ck_ref, keep_ref, got_ref, pp_ref, lm_ref, lg_ref, ud_ref,
                w_ref, rs_ref, a_ref):
    row, z, c = place()
    half = keep_ref.shape[2]
    size = pp_ref.shape[1]
    quarter = size // nz
    mine = pl.ds(pl.multiple_of(c * half, half), half)
    other = pl.ds(pl.multiple_of((1 - c) * half, half), half)
    parent = co_ref[CORES * row + c] // CH
    p_mine, p_other = pp_ref[c, mine, :], pp_ref[c, other, :]
    a_ref[...] = dot(keep_ref[CORES], p_mine) + dot(got_ref[CORES], p_other)
    for p, l_ref in enumerate((lm_ref, lg_ref)):
        j = CORES * z + (c if p == 0 else 1 - c)
        flag = (us_ref[parent, j] * ck_ref[c, j]).astype(F32).astype(BF)
        k_half, g_half = keep_ref[p], got_ref[1 - p]
        w_ref[p] = dot(k_half, p_mine) + dot(g_half, p_other)
        masked = l_ref[...] * flag
        a_ref[mine, :] = a_ref[mine, :] + dot_t(k_half, masked)
        a_ref[other, :] = a_ref[other, :] + dot_t(g_half, masked)
    for s in range(nz):
        block = pl.ds(pl.multiple_of((z ^ s) * quarter, quarter), quarter)
        rs_ref[s, :, :size] = a_ref[block, :].astype(BF)
        rs_ref[s, :, size:] = ud_ref[s]


def lower_body(nz, us_ref, co_ref, ck_ref, to_ref, ts_ref, w_ref, rs1_ref, *refs):
    stacks, (lo_ref, lg_ref, rs_ref, r_ref) = refs[:nz], refs[-4:]
    row, z, c = place()
    quarter = r_ref.shape[0] // nz
    parent = co_ref[CORES * row + c] // CH
    acc = [w_ref[0], w_ref[1]]
    for s in range(nz):
        for q in range(CORES):
            i = CORES * (z ^ s) + (c if q == 0 else 1 - c)
            flag = (us_ref[parent, i] * ck_ref[c, i]).astype(F32).astype(BF)
            piece = stacks[s][q] * flag
            for p, t_ref in enumerate((to_ref, ts_ref)):
                acc[p] = acc[p] + dot(t_ref[i], piece)
    total = None
    for p, o_ref in enumerate((lo_ref, lg_ref)):
        j = CORES * z + (c if p == 0 else 1 - c)
        flag = (us_ref[parent, j] * ck_ref[c, j]).astype(F32)
        block = (-(flag * acc[p])).astype(BF)
        o_ref[...] = block
        prod = dot_t(stacks[0][p], block)
        total = prod if total is None else total + prod
    r_ref[...] = total
    size = r_ref.shape[1]
    for s in range(nz):
        block = pl.ds(pl.multiple_of((z ^ s) * quarter, quarter), quarter)
        rs_ref[s, :, :size] = r_ref[block, :].astype(BF)
        rs_ref[s, :, size:] = rs1_ref[s]


def pair_body(count, *refs):
    for i, ref in enumerate(refs[:count]):
        refs[-1][i] = ref[...]


def order_body(u_own_ref, u_got_ref, l_own_ref, l_got_ref, d_ref, ub_ref, lb_ref, d_out_ref):
    _, _, c = place()
    half = u_own_ref.shape[1]
    own, got = u_own_ref[...], u_got_ref[...]
    ub_ref[0, 0, :, :half] = jnp.where(c == 0, own, got)
    ub_ref[0, 0, :, half:] = jnp.where(c == 0, got, own)
    lb_ref[c, 0] = l_own_ref[...]
    lb_ref[1 - c, 0] = l_got_ref[...]
    d_out_ref[...] = d_ref[...]


def add_body(own_ref, *refs):
    *parts, out_ref = refs
    total = own_ref[0].astype(F32)
    for part in parts:
        total = total + part[...].astype(F32)
    out_ref[...] = total.astype(BF)


def join_body(nz, *refs):
    parts, out_ref = refs[:nz], refs[-1]
    _, z, _ = place()
    for s, part in enumerate(parts):
        quarter = part.shape[0]
        out_ref[pl.ds(pl.multiple_of((z ^ s) * quarter, quarter), quarter), :] = part[...]


def out_body(own_ref, got_ref, d_ref, pp_ref, ld_ref, ud_ref, lp_ref, out_ref):
    _, _, c = place()
    size = pp_ref.shape[1]
    half = size // CORES
    first = own_ref[:, 2 * size :].astype(F32)
    second = got_ref[:, 2 * size :].astype(F32)
    ud_ref[0, :, :half] = d_ref[0, :, :half] + jnp.where(c == 0, first, second)
    ud_ref[0, :, half:] = d_ref[0, :, half:] + jnp.where(c == 0, second, first)
    for k, ref in ((c, own_ref), (1 - c, got_ref)):
        block = -ref[:, size : 2 * size]
        lp_ref[k] = block
        out_ref[k] = ld_ref[k] - dot_t(pp_ref[k], block) - ref[:, :size].astype(F32)


def near_shards(
    rows,
    cols,
    top_inverse,
    upper_structure,
    upper_panels,
    upper_diag_inverse,
    child_order,
    child_keep,
    lower_panels,
    parent_panels,
    lower_diag_inverse,
):
    nz = cols // CORES
    size = upper_panels.shape[-1]
    half, quarter = size // CORES, size // nz
    row, z, c = place()
    first = c == 0

    def over_core(x):
        return lax.ppermute(x, "pcol", [(i, i ^ 1) for i in range(cols)])

    def over_z(x, s):
        return lax.ppermute(x, "pcol", [(i, i ^ (CORES * s)) for i in range(cols)])

    def over_row(x, s):
        return lax.ppermute(x, "prow", [(i, i ^ s) for i in range(rows)])

    shape = jax.ShapeDtypeStruct
    t_own = top_inverse[0]
    u_own = upper_panels[0, 0]
    l_all = lower_panels[:, 0]
    d_own = upper_diag_inverse[0]
    u_sib = over_core(u_own)
    l_own = jnp.where(first, l_all[0], l_all[1])
    l_sib = over_core(jnp.where(first, l_all[1], l_all[0]))
    t_sib = over_core(t_own)
    u_far = [over_z(u_own, s) for s in range(1, nz)]
    u_all = [(u_own, u_sib)] + [(u, over_core(u)) for u in u_far]

    vm = pl.BlockSpec(memory_space=pltpu.VMEM)
    sm = pl.BlockSpec(memory_space=pltpu.SMEM)

    anywhere = pl.BlockSpec(memory_space=pl.ANY)

    def kernel(body, out, args, smem=0, scratch=(), rest=()):
        return pl.pallas_call(
            body,
            out_shape=out,
            in_specs=[sm] * smem + [vm] * (len(args) - smem) + [anywhere] * len(rest),
            out_specs=jax.tree.map(lambda _: vm, out),
            scratch_shapes=list(scratch),
            compiler_params=pltpu.CompilerParams(vmem_limit_bytes=24 * 1024 * 1024),
        )(*args, *rest)

    l_stack = kernel(
        functools.partial(pair_body, 2), shape((CORES, size, size), BF), (l_own, l_sib)
    )
    l_later = lax.optimization_barrier((l_stack, *u_far))[0]
    l_far = [over_z(l_later, s) for s in range(2, nz)]
    scalars = (upper_structure, child_order, child_keep)

    def upper_part(_):
        rx, ud_part = kernel(
            functools.partial(upper_body, nz),
            (shape((CORES + 1, size, half), BF), shape((nz, quarter, half), BF)),
            (upper_structure, t_own, t_sib, *[u for pair in u_all for u in pair]),
            smem=1,
            scratch=[
                pltpu.VMEM((size, half), F32),
                pltpu.VMEM((size, size), F32),
                pltpu.SemaphoreType.DMA,
            ],
            rest=(d_own,),
        )
        rx_all = [rx] + [over_row(rx, s) for s in range(1, rows)]
        keep, give = kernel(
            functools.partial(pick_body, rows),
            (shape(rx.shape, BF), shape(rx.shape, BF)),
            (child_order, *rx_all),
            smem=1,
        )
        got = over_core(give)
        w, rs1 = kernel(
            functools.partial(parent_body, nz),
            (shape((CORES, size, size), F32), shape((nz, quarter, size + half), BF)),
            (*scalars, keep, got, parent_panels, l_own, l_sib, ud_part),
            smem=3,
            scratch=[pltpu.VMEM((size, size), F32)],
        )
        l_next = lax.optimization_barrier((l_stack, rx_all[1]))[0]
        return rx[:CORES], w, rs1, over_z(l_next, 1)

    def no_part(_):
        return (
            jnp.zeros((CORES, size, half), BF),
            jnp.zeros((CORES, size, size), F32),
            jnp.zeros((nz, quarter, size + half), BF),
            jnp.zeros((CORES, size, size), BF),
        )

    ub, w, rs1, l_near = lax.cond(child_order[0] >= 0, upper_part, no_part, None)
    ub_got = over_core(ub[1])
    lb_own, lb_give, sums = kernel(
        functools.partial(lower_body, nz),
        (shape((size, size), BF), shape((size, size), BF), shape((nz, quarter, 2 * size + half), BF)),
        (*scalars, t_own, t_sib, w, rs1, l_stack, l_near, *l_far),
        smem=3,
        scratch=[pltpu.VMEM((size, size), F32)],
    )
    lb_got = over_core(lb_give)
    upper_blocks, lower_blocks, diag = kernel(
        order_body,
        (
            shape((1, 1, size, size), BF),
            shape((CORES, 1, size, size), BF),
            shape((CORES, size, size), F32),
        ),
        (ub[0], ub_got, lb_own, lb_got, lower_diag_inverse),
    )
    got_sums = [over_z(sums[s], s) for s in range(1, nz)]
    part = kernel(add_body, shape(sums.shape[1:], BF), (sums, *got_sums))
    every = [part] + [over_z(part, s) for s in range(1, nz)]
    total = kernel(
        functools.partial(join_body, nz),
        shape((size, part.shape[1]), BF),
        tuple(every),
        rest=(diag,),
    )
    upper_diag, lower_parent, lower_diag = kernel(
        out_body,
        (
            shape((1, size, size), F32),
            shape((CORES, size, size), BF),
            shape((CORES, size, size), F32),
        ),
        (total, over_core(total), upper_diag_inverse, parent_panels, diag),
    )
    return upper_blocks, upper_diag, lower_blocks, lower_parent, lower_diag


def solution(mesh):
    in_specs = (
        P("pcol", None, None, None),
        P(),
        P("prow", "pcol", None, None),
        P("prow", None, None),
        P(),
        P("prow", None),
        P("prow", "pcol", None, None),
        P("prow", None, None),
        P("prow", None, None),
    )
    out_specs = (
        P("prow", "pcol", None, None),
        P("prow", None, None),
        P("prow", "pcol", None, None),
        P("prow", None, None),
        P("prow", None, None),
    )
    rows, cols = mesh.shape["prow"], mesh.shape["pcol"]
    body = functools.partial(near_shards, rows, cols) if cols <= 8 else wide_shards
    return jax.shard_map(body, mesh=mesh, in_specs=in_specs, out_specs=out_specs, check_vma=False)
```

```python
import functools

import jax
import jax.numpy as jnp
from jax import lax
from jax.experimental import pallas as pl
from jax.experimental.pallas import tpu as pltpu
from jax.sharding import PartitionSpec as P

CH = 2
CORES = 2
BF = jnp.bfloat16
F32 = jnp.float32


def dense_sum(top_rows, piece):
    return jnp.einsum("isd,kide->kse", top_rows, piece, preferred_element_type=jnp.float32)


def wide_shards(
    top_inverse,
    upper_structure,
    upper_panels,
    upper_diag_inverse,
    child_order,
    child_keep,
    lower_panels,
    parent_panels,
    lower_diag_inverse,
):
    row_index = lax.axis_index("prow")
    col_index = lax.axis_index("pcol")
    upper_count = upper_panels.shape[0]
    lower_count = lower_panels.shape[0]
    top_rows = top_inverse[0]
    upper_rows = lax.dynamic_slice_in_dim(upper_structure, row_index * upper_count, upper_count, 0)
    upper_flags = lax.dynamic_index_in_dim(upper_rows, col_index, 1, keepdims=False)
    upper_own = upper_panels[:, 0] * upper_flags[:, None, None].astype(jnp.bfloat16)
    order_rows = lax.dynamic_slice_in_dim(child_order, row_index * lower_count, lower_count, 0)
    parent = order_rows // CH
    lower_structure = jnp.take(upper_structure, parent, axis=0) * child_keep
    lower_flags = lax.dynamic_index_in_dim(lower_structure, col_index, 1, keepdims=False)
    lower_own = lower_panels[:, 0] * lower_flags[:, None, None].astype(jnp.bfloat16)
    upper_sum = dense_sum(top_rows, lax.all_gather(upper_own[:, None], "pcol", axis=1, tiled=True))
    upper_local = (-(upper_flags[:, None, None].astype(jnp.float32) * upper_sum)).astype(
        jnp.bfloat16
    )
    diag_term = jnp.einsum(
        "kds,kde->kse", upper_panels[:, 0], upper_local, preferred_element_type=jnp.float32
    )
    own_share = (
        jnp.where(col_index == 0, upper_diag_inverse, jnp.zeros_like(upper_diag_inverse))
        - diag_term
    )
    upper_diag = lax.psum(own_share, "pcol")
    diag_every = lax.all_gather(upper_diag, "prow", axis=0, tiled=True)
    upper_every = lax.all_gather(upper_local, "prow", axis=0, tiled=True)
    lower_sum = dense_sum(top_rows, lax.all_gather(lower_own[:, None], "pcol", axis=1, tiled=True))
    parent_rows = jnp.take(upper_every, parent, axis=0)
    parent_diag = jnp.take(diag_every, parent, axis=0)
    through_parent = jnp.einsum(
        "ksd,kde->kse", parent_rows, parent_panels, preferred_element_type=jnp.float32
    )
    lower_local = (
        -(lower_flags[:, None, None].astype(jnp.float32) * (through_parent + lower_sum))
    ).astype(jnp.bfloat16)
    cross_term = jnp.einsum(
        "kds,kde->kse", parent_rows, lower_own, preferred_element_type=jnp.float32
    )
    lower_term = jnp.einsum(
        "kds,kde->kse", lower_panels[:, 0], lower_local, preferred_element_type=jnp.float32
    )
    cross, lower_total = lax.psum((cross_term, lower_term), "pcol")
    parent_part = jnp.einsum(
        "ksd,kde->kse",
        parent_diag,
        parent_panels.astype(jnp.float32),
        precision=lax.Precision.HIGHEST,
    )
    lower_parent = (-(parent_part + cross)).astype(jnp.bfloat16)
    lower_diag = (
        lower_diag_inverse
        - jnp.einsum(
            "kds,kde->kse", parent_panels, lower_parent, preferred_element_type=jnp.float32
        )
        - lower_total
    )
    return (upper_local[:, None], upper_diag, lower_local[:, None], lower_parent, lower_diag)


def dot(a, b):
    return lax.dot_general(a, b, (((1,), (0,)), ((), ())), preferred_element_type=F32)


def dot_t(a, b):
    return lax.dot_general(a, b, (((0,), (0,)), ((), ())), preferred_element_type=F32)


def place():
    col = lax.axis_index("pcol")
    return lax.axis_index("prow"), col // CORES, col % CORES


def upper_body(nz, us_ref, to_ref, ts_ref, *refs):
    pairs = [(refs[2 * s], refs[2 * s + 1]) for s in range(nz)]
    d_hbm, rx_ref, ud_ref, xs, d_ref, sem = refs[2 * nz :]
    row, z, c = place()
    copy = pltpu.make_async_copy(d_hbm, d_ref, sem)
    copy.start()
    half = xs.shape[1]
    quarter = xs.shape[0] // nz
    acc = [None, None]
    for s in range(nz):
        for q in range(CORES):
            i = CORES * (z ^ s) + (c if q == 0 else 1 - c)
            flag = us_ref[row, i].astype(F32).astype(BF)
            panel = pairs[s][q][...]
            piece = jnp.where(c == 0, panel[:, :half], panel[:, half:]) * flag
            for p, t_ref in enumerate((to_ref, ts_ref)):
                prod = dot(t_ref[i], piece)
                acc[p] = prod if acc[p] is None else acc[p] + prod
    copy.wait()
    x = None
    for p, u_ref in enumerate(pairs[0]):
        j = CORES * z + (c if p == 0 else 1 - c)
        flag = us_ref[row, j].astype(F32)
        block = (-(flag * acc[p])).astype(BF)
        rx_ref[p] = block
        prod = dot_t(u_ref[...], block)
        x = prod if x is None else x + prod
    xs[...] = -x
    for s in range(nz):
        ud_ref[s] = xs[pl.ds(pl.multiple_of((z ^ s) * quarter, quarter), quarter), :].astype(BF)
    own = pl.ds(pl.multiple_of(z * quarter, quarter), quarter)
    rows = d_ref[own, :]
    xs[own, :] = xs[own, :] + jnp.where(c == 0, rows[:, :half], rows[:, half:])
    rx_ref[CORES] = xs[...].astype(BF)


def pick_body(rows, co_ref, *refs):
    blocks, (keep_ref, give_ref) = refs[:rows], refs[-2:]
    row, _, c = place()
    for k, out_ref in ((c, keep_ref), (1 - c, give_ref)):
        index = (co_ref[CORES * row + k] // CH) ^ row
        for s, block in enumerate(blocks):

            @pl.when(index == s)
            def _(out_ref=out_ref, block=block):
                out_ref[...] = block[...]


def parent_body(nz, us_ref, co_ref, ck_ref, keep_ref, got_ref, pp_ref, l_ref, ud_ref,
                w_ref, rs_ref, a_ref):
    row, z, c = place()
    half = keep_ref.shape[2]
    size = pp_ref.shape[1]
    quarter = size // nz
    mine = pl.ds(pl.multiple_of(c * half, half), half)
    other = pl.ds(pl.multiple_of((1 - c) * half, half), half)
    parent = co_ref[CORES * row + c] // CH
    p_mine, p_other = pp_ref[c, mine, :], pp_ref[c, other, :]
    a_ref[...] = dot(keep_ref[CORES], p_mine) + dot(got_ref[CORES], p_other)
    for p in range(CORES):
        j = CORES * z + (c if p == 0 else 1 - c)
        flag = (us_ref[parent, j] * ck_ref[c, j]).astype(F32).astype(BF)
        k_half, g_half = keep_ref[p], got_ref[1 - p]
        w_ref[p] = dot(k_half, p_mine) + dot(g_half, p_other)
        masked = l_ref[p] * flag
        a_ref[mine, :] = a_ref[mine, :] + dot_t(k_half, masked)
        a_ref[other, :] = a_ref[other, :] + dot_t(g_half, masked)
    for s in range(nz):
        block = pl.ds(pl.multiple_of((z ^ s) * quarter, quarter), quarter)
        rs_ref[s, :, :size] = a_ref[block, :].astype(BF)
        rs_ref[s, :, size:] = ud_ref[s]


def lower_body(nz, us_ref, co_ref, ck_ref, to_ref, ts_ref, w_ref, rs1_ref, *refs):
    stacks, (lo_ref, lg_ref, rs_ref, r_ref) = refs[:nz], refs[-4:]
    row, z, c = place()
    quarter = r_ref.shape[0] // nz
    parent = co_ref[CORES * row + c] // CH
    acc = [w_ref[0], w_ref[1]]
    for s in range(nz):
        for q in range(CORES):
            i = CORES * (z ^ s) + (c if q == 0 else 1 - c)
            flag = (us_ref[parent, i] * ck_ref[c, i]).astype(F32).astype(BF)
            piece = stacks[s][q] * flag
            for p, t_ref in enumerate((to_ref, ts_ref)):
                acc[p] = acc[p] + dot(t_ref[i], piece)
    total = None
    for p, o_ref in enumerate((lo_ref, lg_ref)):
        j = CORES * z + (c if p == 0 else 1 - c)
        flag = (us_ref[parent, j] * ck_ref[c, j]).astype(F32)
        block = (-(flag * acc[p])).astype(BF)
        o_ref[...] = block
        prod = dot_t(stacks[0][p], block)
        total = prod if total is None else total + prod
    r_ref[...] = total
    size = r_ref.shape[1]
    for s in range(nz):
        block = pl.ds(pl.multiple_of((z ^ s) * quarter, quarter), quarter)
        rs_ref[s, :, :size] = r_ref[block, :].astype(BF)
        rs_ref[s, :, size:] = rs1_ref[s]


def pair_body(own_ref, got_ref, out_ref):
    _, _, c = place()
    out_ref[0] = own_ref[c]
    out_ref[1] = got_ref[c]


def order_body(u_own_ref, u_got_ref, l_own_ref, l_got_ref, d_ref, ub_ref, lb_ref, d_out_ref):
    _, _, c = place()
    half = u_own_ref.shape[1]
    own, got = u_own_ref[...], u_got_ref[...]
    ub_ref[0, 0, :, :half] = jnp.where(c == 0, own, got)
    ub_ref[0, 0, :, half:] = jnp.where(c == 0, got, own)
    lb_ref[c, 0] = l_own_ref[...]
    lb_ref[1 - c, 0] = l_got_ref[...]
    d_out_ref[...] = d_ref[...]


def add_body(own_ref, *refs):
    *parts, out_ref = refs
    total = own_ref[0].astype(F32)
    for part in parts:
        total = total + part[...].astype(F32)
    out_ref[...] = total.astype(BF)


def join_body(nz, *refs):
    parts, out_ref = refs[:nz], refs[-1]
    _, z, _ = place()
    for s, part in enumerate(parts):
        quarter = part.shape[0]
        out_ref[pl.ds(pl.multiple_of((z ^ s) * quarter, quarter), quarter), :] = part[...]


def out_body(own_ref, got_ref, d_ref, pp_ref, ld_ref, ud_ref, lp_ref, out_ref):
    _, _, c = place()
    size = pp_ref.shape[1]
    half = size // CORES
    first = own_ref[:, 2 * size :].astype(F32)
    second = got_ref[:, 2 * size :].astype(F32)
    ud_ref[0, :, :half] = d_ref[0, :, :half] + jnp.where(c == 0, first, second)
    ud_ref[0, :, half:] = d_ref[0, :, half:] + jnp.where(c == 0, second, first)
    for k, ref in ((c, own_ref), (1 - c, got_ref)):
        block = -ref[:, size : 2 * size]
        lp_ref[k] = block
        out_ref[k] = ld_ref[k] - dot_t(pp_ref[k], block) - ref[:, :size].astype(F32)


def near_shards(
    rows,
    cols,
    top_inverse,
    upper_structure,
    upper_panels,
    upper_diag_inverse,
    child_order,
    child_keep,
    lower_panels,
    parent_panels,
    lower_diag_inverse,
):
    nz = cols // CORES
    size = upper_panels.shape[-1]
    half, quarter = size // CORES, size // nz
    row, z, c = place()

    def over_core(x):
        return lax.ppermute(x, "pcol", [(i, i ^ 1) for i in range(cols)])

    def over_z(x, s):
        return lax.ppermute(x, "pcol", [(i, i ^ (CORES * s)) for i in range(cols)])

    def over_row(x, s):
        return lax.ppermute(x, "prow", [(i, i ^ s) for i in range(rows)])

    shape = jax.ShapeDtypeStruct
    t_own = top_inverse[0]
    u_own = upper_panels[0, 0]
    l_all = lower_panels[:, 0]
    d_own = upper_diag_inverse[0]
    u_sib = over_core(u_own)
    l_got = over_core(l_all)
    t_sib = over_core(t_own)
    u_far = [over_z(u_own, s) for s in range(1, nz)]
    u_all = [(u_own, u_sib)] + [(u, over_core(u)) for u in u_far]

    vm = pl.BlockSpec(memory_space=pltpu.VMEM)
    sm = pl.BlockSpec(memory_space=pltpu.SMEM)

    anywhere = pl.BlockSpec(memory_space=pl.ANY)

    def kernel(body, out, args, smem=0, scratch=(), rest=()):
        return pl.pallas_call(
            body,
            out_shape=out,
            in_specs=[sm] * smem + [vm] * (len(args) - smem) + [anywhere] * len(rest),
            out_specs=jax.tree.map(lambda _: vm, out),
            scratch_shapes=list(scratch),
            compiler_params=pltpu.CompilerParams(vmem_limit_bytes=24 * 1024 * 1024),
        )(*args, *rest)

    l_stack = kernel(pair_body, shape((CORES, size, size), BF), (l_all, l_got))
    l_later = lax.optimization_barrier((l_stack, *u_far))[0]
    l_far = [over_z(l_later, s) for s in range(1, nz)]
    scalars = (upper_structure, child_order, child_keep)

    def upper_part(_):
        rx, ud_part = kernel(
            functools.partial(upper_body, nz),
            (shape((CORES + 1, size, half), BF), shape((nz, quarter, half), BF)),
            (upper_structure, t_own, t_sib, *[u for pair in u_all for u in pair]),
            smem=1,
            scratch=[
                pltpu.VMEM((size, half), F32),
                pltpu.VMEM((size, size), F32),
                pltpu.SemaphoreType.DMA,
            ],
            rest=(d_own,),
        )
        rx_all = [rx]
        for s in range(1, rows):
            rx_all.append(over_row(rx_all[s & (s - 1)], s & -s))
        keep, give = kernel(
            functools.partial(pick_body, rows),
            (shape(rx.shape, BF), shape(rx.shape, BF)),
            (child_order, *rx_all),
            smem=1,
        )
        got = over_core(give)
        w, rs1 = kernel(
            functools.partial(parent_body, nz),
            (shape((CORES, size, size), F32), shape((nz, quarter, size + half), BF)),
            (*scalars, keep, got, parent_panels, l_stack, ud_part),
            smem=3,
            scratch=[pltpu.VMEM((size, size), F32)],
        )
        return rx[:CORES], w, rs1

    def no_part(_):
        return (
            jnp.zeros((CORES, size, half), BF),
            jnp.zeros((CORES, size, size), F32),
            jnp.zeros((nz, quarter, size + half), BF),
        )

    ub, w, rs1 = lax.cond(row >= 0, upper_part, no_part, None)
    ub_got = over_core(ub[1])
    lb_own, lb_give, sums = kernel(
        functools.partial(lower_body, nz),
        (shape((size, size), BF), shape((size, size), BF), shape((nz, quarter, 2 * size + half), BF)),
        (*scalars, t_own, t_sib, w, rs1, l_stack, *l_far),
        smem=3,
        scratch=[pltpu.VMEM((size, size), F32)],
    )
    lb_got = over_core(lb_give)
    upper_blocks, lower_blocks, diag = kernel(
        order_body,
        (
            shape((1, 1, size, size), BF),
            shape((CORES, 1, size, size), BF),
            shape((CORES, size, size), F32),
        ),
        (ub[0], ub_got, lb_own, lb_got, lower_diag_inverse),
    )
    got_sums = [over_z(sums[s], s) for s in range(1, nz)]
    part = kernel(add_body, shape(sums.shape[1:], BF), (sums, *got_sums))
    every = [part] + [over_z(part, s) for s in range(1, nz)]
    total = kernel(
        functools.partial(join_body, nz),
        shape((size, part.shape[1]), BF),
        tuple(every),
        rest=(diag,),
    )
    upper_diag, lower_parent, lower_diag = kernel(
        out_body,
        (
            shape((1, size, size), F32),
            shape((CORES, size, size), BF),
            shape((CORES, size, size), F32),
        ),
        (total, over_core(total), upper_diag_inverse, parent_panels, diag),
    )
    return upper_blocks, upper_diag, lower_blocks, lower_parent, lower_diag


def solution(mesh):
    in_specs = (
        P("pcol", None, None, None),
        P(),
        P("prow", "pcol", None, None),
        P("prow", None, None),
        P(),
        P("prow", None),
        P("prow", "pcol", None, None),
        P("prow", None, None),
        P("prow", None, None),
    )
    out_specs = (
        P("prow", "pcol", None, None),
        P("prow", None, None),
        P("prow", "pcol", None, None),
        P("prow", None, None),
        P("prow", None, None),
    )
    rows, cols = mesh.shape["prow"], mesh.shape["pcol"]
    body = functools.partial(near_shards, rows, cols) if cols <= 8 else wide_shards
    return jax.shard_map(body, mesh=mesh, in_specs=in_specs, out_specs=out_specs, check_vma=False)
```

```python
import functools

import jax
import jax.numpy as jnp
from jax import lax
from jax.experimental import pallas as pl
from jax.experimental.pallas import tpu as pltpu
from jax.sharding import PartitionSpec as P

CH = 2
CORES = 2
BF = jnp.bfloat16
F32 = jnp.float32


def dense_sum(top_rows, piece):
    return jnp.einsum("isd,kide->kse", top_rows, piece, preferred_element_type=jnp.float32)


def wide_shards(
    top_inverse,
    upper_structure,
    upper_panels,
    upper_diag_inverse,
    child_order,
    child_keep,
    lower_panels,
    parent_panels,
    lower_diag_inverse,
):
    row_index = lax.axis_index("prow")
    col_index = lax.axis_index("pcol")
    upper_count = upper_panels.shape[0]
    lower_count = lower_panels.shape[0]
    top_rows = top_inverse[0]
    upper_rows = lax.dynamic_slice_in_dim(upper_structure, row_index * upper_count, upper_count, 0)
    upper_flags = lax.dynamic_index_in_dim(upper_rows, col_index, 1, keepdims=False)
    upper_own = upper_panels[:, 0] * upper_flags[:, None, None].astype(jnp.bfloat16)
    order_rows = lax.dynamic_slice_in_dim(child_order, row_index * lower_count, lower_count, 0)
    parent = order_rows // CH
    lower_structure = jnp.take(upper_structure, parent, axis=0) * child_keep
    lower_flags = lax.dynamic_index_in_dim(lower_structure, col_index, 1, keepdims=False)
    lower_own = lower_panels[:, 0] * lower_flags[:, None, None].astype(jnp.bfloat16)
    upper_sum = dense_sum(top_rows, lax.all_gather(upper_own[:, None], "pcol", axis=1, tiled=True))
    upper_local = (-(upper_flags[:, None, None].astype(jnp.float32) * upper_sum)).astype(
        jnp.bfloat16
    )
    diag_term = jnp.einsum(
        "kds,kde->kse", upper_panels[:, 0], upper_local, preferred_element_type=jnp.float32
    )
    own_share = (
        jnp.where(col_index == 0, upper_diag_inverse, jnp.zeros_like(upper_diag_inverse))
        - diag_term
    )
    upper_diag = lax.psum(own_share, "pcol")
    diag_every = lax.all_gather(upper_diag, "prow", axis=0, tiled=True)
    upper_every = lax.all_gather(upper_local, "prow", axis=0, tiled=True)
    lower_sum = dense_sum(top_rows, lax.all_gather(lower_own[:, None], "pcol", axis=1, tiled=True))
    parent_rows = jnp.take(upper_every, parent, axis=0)
    parent_diag = jnp.take(diag_every, parent, axis=0)
    through_parent = jnp.einsum(
        "ksd,kde->kse", parent_rows, parent_panels, preferred_element_type=jnp.float32
    )
    lower_local = (
        -(lower_flags[:, None, None].astype(jnp.float32) * (through_parent + lower_sum))
    ).astype(jnp.bfloat16)
    cross_term = jnp.einsum(
        "kds,kde->kse", parent_rows, lower_own, preferred_element_type=jnp.float32
    )
    lower_term = jnp.einsum(
        "kds,kde->kse", lower_panels[:, 0], lower_local, preferred_element_type=jnp.float32
    )
    cross, lower_total = lax.psum((cross_term, lower_term), "pcol")
    parent_part = jnp.einsum(
        "ksd,kde->kse",
        parent_diag,
        parent_panels.astype(jnp.float32),
        precision=lax.Precision.HIGHEST,
    )
    lower_parent = (-(parent_part + cross)).astype(jnp.bfloat16)
    lower_diag = (
        lower_diag_inverse
        - jnp.einsum(
            "kds,kde->kse", parent_panels, lower_parent, preferred_element_type=jnp.float32
        )
        - lower_total
    )
    return (upper_local[:, None], upper_diag, lower_local[:, None], lower_parent, lower_diag)


def dot(a, b):
    return lax.dot_general(a, b, (((1,), (0,)), ((), ())), preferred_element_type=F32)


def dot_t(a, b):
    return lax.dot_general(a, b, (((0,), (0,)), ((), ())), preferred_element_type=F32)


def place():
    col = lax.axis_index("pcol")
    return lax.axis_index("prow"), col // CORES, col % CORES


def upper_body(nz, flags_ref, to_ref, ts_ref, *refs):
    pairs = [(refs[2 * s], refs[2 * s + 1]) for s in range(nz)]
    d_hbm, rx_ref, ud_ref, xs, d_ref, sem = refs[2 * nz :]
    row, z, c = place()
    copy = pltpu.make_async_copy(d_hbm, d_ref, sem)
    copy.start()
    half = xs.shape[1]
    quarter = xs.shape[0] // nz
    acc = [None, None]
    for s in range(nz):
        for q in range(CORES):
            i = CORES * (z ^ s) + (c if q == 0 else 1 - c)
            flag = flags_ref[pl.ds(CORES * s + q, 1), :half].astype(BF)
            panel = pairs[s][q][...]
            piece = jnp.where(c == 0, panel[:, :half], panel[:, half:]) * flag
            for p, t_ref in enumerate((to_ref, ts_ref)):
                prod = dot(t_ref[i], piece)
                acc[p] = prod if acc[p] is None else acc[p] + prod
    copy.wait()
    x = None
    for p, u_ref in enumerate(pairs[0]):
        flag = flags_ref[pl.ds(p, 1), :half]
        block = (-(flag * acc[p])).astype(BF)
        rx_ref[p] = block
        prod = dot_t(u_ref[...], block)
        x = prod if x is None else x + prod
    xs[...] = -x
    for s in range(nz):
        ud_ref[s] = xs[pl.ds(pl.multiple_of((z ^ s) * quarter, quarter), quarter), :].astype(BF)
    own = pl.ds(pl.multiple_of(z * quarter, quarter), quarter)
    rows = d_ref[own, :]
    xs[own, :] = xs[own, :] + jnp.where(c == 0, rows[:, :half], rows[:, half:])
    rx_ref[CORES] = xs[...].astype(BF)


def pick_body(nz, rows, flags_ref, *refs):
    blocks, outs = refs[:rows], refs[-2:]
    half = outs[0].shape[2]
    for k, out_ref in enumerate(outs):
        total = None
        for s, block in enumerate(blocks):
            flag = flags_ref[pl.ds(2 * CORES * nz + rows * k + s, 1), :half].astype(BF)
            part = block[...] * flag
            total = part if total is None else total + part
        out_ref[...] = total


def parent_body(nz, flags_ref, keep_ref, got_ref, pp_ref, l_ref, ud_ref,
                w_ref, rs_ref, a_ref):
    _, z, c = place()
    half = keep_ref.shape[2]
    size = pp_ref.shape[1]
    quarter = size // nz
    mine = pl.ds(pl.multiple_of(c * half, half), half)
    other = pl.ds(pl.multiple_of((1 - c) * half, half), half)
    p_mine, p_other = pp_ref[c, mine, :], pp_ref[c, other, :]
    a_ref[...] = dot(keep_ref[CORES], p_mine) + dot(got_ref[CORES], p_other)
    for p in range(CORES):
        flag = flags_ref[pl.ds(CORES * nz + p, 1), :].astype(BF)
        k_half, g_half = keep_ref[p], got_ref[1 - p]
        w_ref[p] = dot(k_half, p_mine) + dot(g_half, p_other)
        masked = l_ref[p] * flag
        a_ref[mine, :] = a_ref[mine, :] + dot_t(k_half, masked)
        a_ref[other, :] = a_ref[other, :] + dot_t(g_half, masked)
    for s in range(nz):
        block = pl.ds(pl.multiple_of((z ^ s) * quarter, quarter), quarter)
        rs_ref[s, :, :size] = a_ref[block, :].astype(BF)
        rs_ref[s, :, size:] = ud_ref[s]


def lower_body(nz, flags_ref, to_ref, ts_ref, w_ref, rs1_ref, *refs):
    stacks, (lo_ref, lg_ref, rs_ref, r_ref) = refs[:nz], refs[-4:]
    _, z, c = place()
    quarter = r_ref.shape[0] // nz
    acc = [w_ref[0], w_ref[1]]
    for s in range(nz):
        for q in range(CORES):
            i = CORES * (z ^ s) + (c if q == 0 else 1 - c)
            flag = flags_ref[pl.ds(CORES * nz + CORES * s + q, 1), :].astype(BF)
            piece = stacks[s][q] * flag
            for p, t_ref in enumerate((to_ref, ts_ref)):
                acc[p] = acc[p] + dot(t_ref[i], piece)
    total = None
    for p, o_ref in enumerate((lo_ref, lg_ref)):
        flag = flags_ref[pl.ds(CORES * nz + p, 1), :]
        block = (-(flag * acc[p])).astype(BF)
        o_ref[...] = block
        prod = dot_t(stacks[0][p], block)
        total = prod if total is None else total + prod
    r_ref[...] = total
    size = r_ref.shape[1]
    for s in range(nz):
        block = pl.ds(pl.multiple_of((z ^ s) * quarter, quarter), quarter)
        rs_ref[s, :, :size] = r_ref[block, :].astype(BF)
        rs_ref[s, :, size:] = rs1_ref[s]


def pair_body(own_ref, got_ref, _, out_ref):
    c = place()[2]
    out_ref[0] = own_ref[c]
    out_ref[1] = got_ref[c]


def flags_body(nz, rows, us_ref, co_ref, ck_ref, flags_ref):
    row, z, c = place()
    parents = [co_ref[CORES * row + k] // CH for k in (c, 1 - c)]
    places = [CORES * (z ^ s) + (c if q == 0 else 1 - c) for s in range(nz) for q in range(CORES)]
    flags = [us_ref[row, i] for i in places]
    flags += [us_ref[parents[0], i] * ck_ref[c, i] for i in places]
    for parent in parents:
        flags += [jnp.where((parent ^ row) == s, 1, 0) for s in range(rows)]
    for n, flag in enumerate(flags):
        flags_ref[pl.ds(n, 1), :] = jnp.full((1, flags_ref.shape[1]), flag, jnp.int32).astype(F32)


def order_body(u_own_ref, u_got_ref, l_own_ref, l_got_ref, d_ref, ub_ref, lb_ref, d_out_ref):
    _, _, c = place()
    half = u_own_ref.shape[1]
    own, got = u_own_ref[...], u_got_ref[...]
    ub_ref[0, 0, :, :half] = jnp.where(c == 0, own, got)
    ub_ref[0, 0, :, half:] = jnp.where(c == 0, got, own)
    lb_ref[c, 0] = l_own_ref[...]
    lb_ref[1 - c, 0] = l_got_ref[...]
    d_out_ref[...] = d_ref[...]


def add_body(own_ref, *refs):
    *parts, out_ref = refs
    total = own_ref[0].astype(F32)
    for part in parts:
        total = total + part[...].astype(F32)
    out_ref[...] = total.astype(BF)


def join_body(nz, *refs):
    parts, out_ref = refs[:nz], refs[-1]
    _, z, _ = place()
    for s, part in enumerate(parts):
        quarter = part.shape[0]
        out_ref[pl.ds(pl.multiple_of((z ^ s) * quarter, quarter), quarter), :] = part[...]


def out_body(own_ref, got_ref, d_ref, pp_ref, ld_ref, ud_ref, lp_ref, out_ref):
    _, _, c = place()
    size = pp_ref.shape[1]
    half = size // CORES
    first = own_ref[:, 2 * size :].astype(F32)
    second = got_ref[:, 2 * size :].astype(F32)
    ud_ref[0, :, :half] = d_ref[0, :, :half] + jnp.where(c == 0, first, second)
    ud_ref[0, :, half:] = d_ref[0, :, half:] + jnp.where(c == 0, second, first)
    for k, ref in ((c, own_ref), (1 - c, got_ref)):
        block = -ref[:, size : 2 * size]
        lp_ref[k] = block
        out_ref[k] = ld_ref[k] - dot_t(pp_ref[k], block) - ref[:, :size].astype(F32)


def near_shards(
    rows,
    cols,
    top_inverse,
    upper_structure,
    upper_panels,
    upper_diag_inverse,
    child_order,
    child_keep,
    lower_panels,
    parent_panels,
    lower_diag_inverse,
):
    nz = cols // CORES
    size = upper_panels.shape[-1]
    half, quarter = size // CORES, size // nz
    row, z, c = place()

    def over_core(x):
        return lax.ppermute(x, "pcol", [(i, i ^ 1) for i in range(cols)])

    def over_z(x, s):
        return lax.ppermute(x, "pcol", [(i, i ^ (CORES * s)) for i in range(cols)])

    def over_row(x, s):
        return lax.ppermute(x, "prow", [(i, i ^ s) for i in range(rows)])

    shape = jax.ShapeDtypeStruct
    t_own = top_inverse[0]
    u_own = upper_panels[0, 0]
    l_all = lower_panels[:, 0]
    d_own = upper_diag_inverse[0]
    u_sib = over_core(u_own)
    l_got = over_core(l_all)
    t_sib = over_core(t_own)
    u_far = [over_z(u_own, s) for s in range(1, nz)]
    u_all = [(u_own, u_sib)] + [(u, over_core(u)) for u in u_far]

    vm = pl.BlockSpec(memory_space=pltpu.VMEM)
    sm = pl.BlockSpec(memory_space=pltpu.SMEM)

    anywhere = pl.BlockSpec(memory_space=pl.ANY)

    def kernel(body, out, args, smem=0, scratch=(), rest=()):
        return pl.pallas_call(
            body,
            out_shape=out,
            in_specs=[sm] * smem + [vm] * (len(args) - smem) + [anywhere] * len(rest),
            out_specs=jax.tree.map(lambda _: vm, out),
            scratch_shapes=list(scratch),
            compiler_params=pltpu.CompilerParams(vmem_limit_bytes=24 * 1024 * 1024),
        )(*args, *rest)

    scalars = (upper_structure, child_order, child_keep)
    flags = kernel(
        functools.partial(flags_body, nz, rows),
        shape((2 * CORES * nz + CORES * rows, size), F32),
        scalars,
        smem=3,
    )
    l_stack = kernel(
        pair_body, shape((CORES, size, size), BF), (l_all, l_got), rest=(flags,)
    )
    l_later = lax.optimization_barrier((l_stack, *u_far))[0]
    l_far = [over_z(l_later, s) for s in range(1, nz)]

    def upper_part(_):
        rx, ud_part = kernel(
            functools.partial(upper_body, nz),
            (shape((CORES + 1, size, half), BF), shape((nz, quarter, half), BF)),
            (flags, t_own, t_sib, *[u for pair in u_all for u in pair]),
            scratch=[
                pltpu.VMEM((size, half), F32),
                pltpu.VMEM((size, size), F32),
                pltpu.SemaphoreType.DMA,
            ],
            rest=(d_own,),
        )
        rx_all = [rx]
        for s in range(1, rows):
            rx_all.append(over_row(rx_all[s & (s - 1)], s & -s))
        keep, give = kernel(
            functools.partial(pick_body, nz, rows),
            (shape(rx.shape, BF), shape(rx.shape, BF)),
            (flags, *rx_all),
        )
        got = over_core(give)
        w, rs1 = kernel(
            functools.partial(parent_body, nz),
            (shape((CORES, size, size), F32), shape((nz, quarter, size + half), BF)),
            (flags, keep, got, parent_panels, l_stack, ud_part),
            scratch=[pltpu.VMEM((size, size), F32)],
        )
        return rx[:CORES], w, rs1

    def no_part(_):
        return (
            jnp.zeros((CORES, size, half), BF),
            jnp.zeros((CORES, size, size), F32),
            jnp.zeros((nz, quarter, size + half), BF),
        )

    ub, w, rs1 = lax.cond(row >= 0, upper_part, no_part, None)
    ub_got = over_core(ub[1])
    lb_own, lb_give, sums = kernel(
        functools.partial(lower_body, nz),
        (shape((size, size), BF), shape((size, size), BF), shape((nz, quarter, 2 * size + half), BF)),
        (flags, t_own, t_sib, w, rs1, l_stack, *l_far),
        scratch=[pltpu.VMEM((size, size), F32)],
    )
    lb_got = over_core(lb_give)
    upper_blocks, lower_blocks, diag = kernel(
        order_body,
        (
            shape((1, 1, size, size), BF),
            shape((CORES, 1, size, size), BF),
            shape((CORES, size, size), F32),
        ),
        (ub[0], ub_got, lb_own, lb_got, lower_diag_inverse),
    )
    got_sums = [over_z(sums[s], s) for s in range(1, nz)]
    part = kernel(add_body, shape(sums.shape[1:], BF), (sums, *got_sums))
    every = [part] + [over_z(part, s) for s in range(1, nz)]
    total = kernel(
        functools.partial(join_body, nz),
        shape((size, part.shape[1]), BF),
        tuple(every),
        rest=(diag,),
    )
    upper_diag, lower_parent, lower_diag = kernel(
        out_body,
        (
            shape((1, size, size), F32),
            shape((CORES, size, size), BF),
            shape((CORES, size, size), F32),
        ),
        (total, over_core(total), upper_diag_inverse, parent_panels, diag),
    )
    return upper_blocks, upper_diag, lower_blocks, lower_parent, lower_diag


def solution(mesh):
    in_specs = (
        P("pcol", None, None, None),
        P(),
        P("prow", "pcol", None, None),
        P("prow", None, None),
        P(),
        P("prow", None),
        P("prow", "pcol", None, None),
        P("prow", None, None),
        P("prow", None, None),
    )
    out_specs = (
        P("prow", "pcol", None, None),
        P("prow", None, None),
        P("prow", "pcol", None, None),
        P("prow", None, None),
        P("prow", None, None),
    )
    rows, cols = mesh.shape["prow"], mesh.shape["pcol"]
    body = functools.partial(near_shards, rows, cols) if cols <= 8 else wide_shards
    return jax.shard_map(body, mesh=mesh, in_specs=in_specs, out_specs=out_specs, check_vma=False)
```
